32 devices in a mesh: row: 4 (over y, x), col: 8 (over z, core).
Axes of the slice: x: 2, y: 2, z: 4, core: 2. Of those that a mesh axis runs over, the one named last changes fastest.
Arguments:
- features: bfloat16 [4096, 256], P(('col', 'row')), may hold values from -6 to 6
- weight: bfloat16 [256, 256], replicated, may hold values from -0.375 to 0.375
- bias_term: float32 [256], replicated, may hold values from -3 to 3
- block_values: bfloat16 [4, 8, 16, 128, 128], P('row', 'col'), may hold values from -0.21875 to 0.21875
- block_rows: int32 [4, 8, 16], P('row', 'col'), may hold values from 0 to 7, as said below
- block_cols: int32 [4, 8, 16], P('row', 'col'), may hold values from 0 to 3, as said below
- counts: int32 [4, 8], P('row', 'col'), may hold values from 1 to 16, as said below
- cluster_order: int32 [4096], P('col'), may hold values from 0 to 511, as said below
- cotangent: bfloat16 [4096, 256], P(('row', 'col')), may hold values from -6 to 6
Outputs:
- activations: bfloat16 [4096, 256], P(('row', 'col'))
- grad_features: bfloat16 [4096, 256], P(('col', 'row'))
- grad_weight: float32 [256, 256], replicated
The draws below stay inside these ranges and needn't reach their ends.
Inputs may be any that keep to these rules, and one draw needn't show every extreme that they name: Slots from counts on are ignored; some tile holds 16 live slots. `block_rows`: within one tile, the slots name distinct pairs of block row and block column. `block_cols`: paired with block_rows as stated there. `cluster_order`: each run of 512 entries that starts at a multiple of 512 is a permutation of 0 to 511.
All inputs are finite; a program needn't handle non-finite values.
Results may differ from the reference program's by a relative error of at most 0.015.
Values may be sent and summed in bfloat16 or wider, within the bound.
No kernel may reach another device: no remote copies, remote signals or barrier semaphores. Data moves between devices by JAX's collectives and lax.ppermute only.
A program may use at most 64 MiB of HBM per device.

```python
import math
import jax
import jax.numpy as jnp
from jax import lax

F = 256
BLK = 128
NODES = 4096
ROWNODES = 1024
COLNODES = 512
ROWBLK = 8
COLBLK = 4
CAP = 16
N_ROW = 4
N_COL = 8


def tile_positions(key):
    tile_keys = jax.random.split(key, N_ROW * N_COL)
    positions = jax.vmap(lambda one_key: jax.random.permutation(one_key, ROWBLK * COLBLK)[:CAP])(tile_keys)
    return positions.reshape(N_ROW, N_COL, CAP).astype(jnp.int32)


def draw_block_rows(key, part):
    positions = tile_positions(key)
    return (positions // COLBLK).astype(jnp.int32)


def draw_block_cols(key, part):
    positions = tile_positions(key)
    return (positions % COLBLK).astype(jnp.int32)


def draw_counts(key, part):
    key = jax.random.fold_in(key, 3)
    first_key, second_key = jax.random.split(key)
    factor = jax.random.randint(first_key, (N_ROW, N_COL), 1, 65)
    filled = jnp.maximum(CAP * factor * factor // 4096, 1)
    chosen = jax.random.randint(second_key, (), 0, N_ROW * N_COL)
    filled = filled.reshape(-1).at[chosen].set(CAP).reshape(N_ROW, N_COL)
    return filled.astype(jnp.int32)


def draw_cluster_order(key, part):
    key = jax.random.fold_in(key, 4)
    group_keys = jax.random.split(key, N_COL)
    orders = jax.vmap(lambda one_key: jax.random.permutation(one_key, COLNODES))(group_keys)
    return orders.reshape(NODES).astype(jnp.int32)


def levels(rng, shape, cuts, low, high):
    factor_of, own = 1.0, jax.random.fold_in(rng, 6)
    for position, blocks in cuts:
        steps = jnp.exp(jax.random.uniform(jax.random.fold_in(own, position), (blocks,), jnp.float32, low / len(cuts), high / len(cuts)))
        factor_of = factor_of * jnp.repeat(steps, shape[position] // blocks).reshape([-1 if axis == position else 1 for axis in range(len(shape))])
    return factor_of


def scatter_about(key, dims, spread, reach, shards=(), kind=jnp.bfloat16):
    result = spread * jax.random.normal(key, dims, jnp.float32)
    if shards:
        result = result * levels(key, dims, shards, -0.22, 0.18)
    return jnp.clip(result, -reach, reach).astype(kind)


def setup_inputs(seed: int = 0) -> dict:
    arg_keys = jax.random.split(jax.random.key(seed), 10)
    return {
        "features": scatter_about(arg_keys[0], (NODES, F), 1.0, 6.0, ((0, 32),)),
        "weight": scatter_about(arg_keys[1], (F, F), F ** -0.5, 0.375),
        "bias_term": scatter_about(arg_keys[2], (F,), 0.5, 3.0, (), jnp.float32),
        "block_values": scatter_about(arg_keys[3], (N_ROW, N_COL, CAP, BLK, BLK), (max(CAP * N_COL * BLK // (3 * ROWBLK), 1)) ** -0.5, 0.21875, ((0, 4), (1, 8))),
        "block_rows": draw_block_rows(jax.random.fold_in(arg_keys[9], 71), 0),
        "block_cols": draw_block_cols(jax.random.fold_in(arg_keys[9], 71), 0),
        "counts": draw_counts(jax.random.fold_in(arg_keys[9], 71), 0),
        "cluster_order": draw_cluster_order(jax.random.fold_in(arg_keys[9], 71), 0),
        "cotangent": scatter_about(arg_keys[8], (NODES, F), 1.0, 6.0, ((0, 32),)),
    }


def silu_slope(preact):
    sigmoid_value = jax.nn.sigmoid(preact)
    return sigmoid_value * (1.0 + preact * (1.0 - sigmoid_value))

def reference(features, weight, bias_term, block_values, block_rows, block_cols, counts, cluster_order, cotangent):
    hidden = jnp.dot(features, weight, preferred_element_type=jnp.float32).astype(jnp.bfloat16)
    column_groups = hidden.reshape(N_COL, COLNODES, F)
    local_order = cluster_order.reshape(N_COL, COLNODES)
    slot_ids = jnp.arange(CAP, dtype=jnp.int32)

    def forward_tile(row_id, col_id):
        group_rows = column_groups[col_id][local_order[col_id]]
        gathered = group_rows.reshape(COLBLK, BLK, F)[block_cols[row_id, col_id]]
        product = jnp.einsum('sij,sjf->sif', block_values[row_id, col_id].astype(jnp.float32), gathered.astype(jnp.float32))
        active = (slot_ids < counts[row_id, col_id]).astype(jnp.float32)
        partial_sum = jax.ops.segment_sum(product * active[:, None, None], block_rows[row_id, col_id], num_segments=ROWBLK)
        return partial_sum.reshape(ROWNODES, F)

    def forward_row(row_id):

        def accumulate(running, col_id):
            rounded = lax.optimization_barrier(forward_tile(row_id, col_id).astype(jnp.bfloat16))
            return (running + rounded.astype(jnp.float32), None)
        running, _ = lax.scan(accumulate, jnp.zeros((ROWNODES, F), jnp.float32), jnp.arange(N_COL, dtype=jnp.int32))
        return running
    summed = lax.map(forward_row, jnp.arange(N_ROW, dtype=jnp.int32)).reshape(NODES, F)
    preact = summed + bias_term
    activations = jax.nn.silu(preact).astype(jnp.bfloat16)
    slopes = (cotangent.astype(jnp.float32) * silu_slope(preact)).astype(jnp.bfloat16)
    slope_groups = slopes.reshape(N_ROW, ROWNODES, F)

    def backward_tile(row_id, col_id):
        gathered = slope_groups[row_id].reshape(ROWBLK, BLK, F)[block_rows[row_id, col_id]]
        product = jnp.einsum('sij,sif->sjf', block_values[row_id, col_id].astype(jnp.float32), gathered.astype(jnp.float32))
        active = (slot_ids < counts[row_id, col_id]).astype(jnp.float32)
        partial_sum = jax.ops.segment_sum(product * active[:, None, None], block_cols[row_id, col_id], num_segments=COLBLK)
        cluster_terms = partial_sum.reshape(COLNODES, F)
        return jnp.zeros((COLNODES, F), jnp.float32).at[local_order[col_id]].set(cluster_terms)

    def backward_col(col_id):

        def accumulate(running, row_id):
            rounded = lax.optimization_barrier(backward_tile(row_id, col_id).astype(jnp.bfloat16))
            return (running + rounded.astype(jnp.float32), None)
        running, _ = lax.scan(accumulate, jnp.zeros((COLNODES, F), jnp.float32), jnp.arange(N_ROW, dtype=jnp.int32))
        return running
    grad_sum = lax.map(backward_col, jnp.arange(N_COL, dtype=jnp.int32)).reshape(NODES, F)
    grad_hidden = grad_sum.astype(jnp.bfloat16)
    grad_features = jnp.dot(grad_hidden, weight.T, preferred_element_type=jnp.float32).astype(jnp.bfloat16)
    grad_weight = jnp.dot(features.T, grad_hidden, preferred_element_type=jnp.float32) / math.sqrt(NODES)
    return (activations, grad_features, grad_weight)
```

```python
import functools
import math

import jax
import jax.numpy as jnp
from jax import lax
from jax.experimental import pallas as pl
from jax.experimental.pallas import tpu as pltpu
from jax.sharding import PartitionSpec as P

F32 = jnp.float32
BF16 = jnp.bfloat16
VMEM_LIMIT = 48 * 1024 * 1024


def params():
    return pltpu.CompilerParams(vmem_limit_bytes=VMEM_LIMIT)


def cost(flops, nbytes, transcendentals=0):
    return pl.CostEstimate(flops=flops, bytes_accessed=nbytes, transcendentals=transcendentals)


def whole(shape):
    return pl.BlockSpec(shape, lambda *_: (0,) * len(shape))


def swap(value, axis, mask):
    size = lax.axis_size(axis)
    return lax.ppermute(value, axis, [(i, i ^ mask) for i in range(size)])


def tiled_dot(shape, store, lhs_rows, rhs_rows):
    rows, cols = shape
    row_step, col_step = min(rows, 512), min(cols, 512)

    def tile(i, j):
        left = lhs_rows(pl.multiple_of(i * row_step, row_step), row_step)
        right = rhs_rows(pl.multiple_of(j * col_step, col_step), col_step)
        return lax.dot_general(left, right, NT, preferred_element_type=F32)

    def step(t, carry):
        i, j = t // (cols // col_step), t % (cols // col_step)
        value = tile(i, j)
        rows_at = pl.ds(pl.multiple_of(i * row_step, row_step), row_step)
        store(rows_at, pl.ds(pl.multiple_of(j * col_step, col_step), col_step), value)
        return carry

    steps = (rows // row_step) * (cols // col_step)
    if steps <= 4:
        for t in range(steps):
            step(t, 0)
    else:
        lax.fori_loop(0, steps, step, 0)


NT = (((1,), (1,)), ((), ()))


def prep_kernel(per_step, rows_ref, cols_ref, count_ref, order_ref, values_ref, a_ref, at_ref, dense, select):
    block = values_ref.shape[1]
    nodes = select.shape[0]
    first = pl.program_id(0) * per_step
    row_blocks = pl.num_programs(0) * per_step
    row, col = lax.axis_index("row"), lax.axis_index("col")

    dense[...] = jnp.zeros_like(dense)
    local = lax.broadcasted_iota(jnp.int32, (block, block), 0)
    for chunk in range(nodes // block):
        node = (row ^ chunk) * block + local
        for part in range(nodes // block):
            hit = order_ref[part : part + 1, :] == node
            select[chunk * block : (chunk + 1) * block, part * block : (part + 1) * block] = jnp.where(
                hit, 1.0, 0.0
            ).astype(BF16)

    def slot(s, carry):
        turned = rows_ref[s] ^ col
        place = (turned & 1) * (row_blocks // 2) + (turned >> 1) - first

        @pl.when((place >= 0) & (place < per_step))
        def _():
            dense[
                pl.ds(pl.multiple_of(place * block, block), block),
                pl.ds(pl.multiple_of(cols_ref[s] * block, block), block),
            ] = values_ref[s]

        return carry

    lax.fori_loop(0, count_ref[0], slot, 0)

    def store_a(i, j, value):
        a_ref[i, j] = value.astype(BF16)

    def store_at(i, j, value):
        at_ref[i, j] = value.astype(BF16)

    dense_rows = lambda i, n: dense[pl.ds(i, n), :]
    select_rows = lambda i, n: select[pl.ds(i, n), :]
    tiled_dot((per_step * block, nodes), store_a, dense_rows, select_rows)
    tiled_dot((nodes, per_step * block), store_at, select_rows, dense_rows)


def prep(values, rows, cols, count, order, row_blocks):
    capacity, block, _ = values.shape
    nodes = order.shape[0]
    per_step = min(row_blocks, 8)
    smem = pl.BlockSpec(memory_space=pltpu.SMEM)
    return pl.pallas_call(
        functools.partial(prep_kernel, per_step),
        grid=(row_blocks // per_step,),
        out_shape=(
            jax.ShapeDtypeStruct((row_blocks * block, nodes), BF16),
            jax.ShapeDtypeStruct((nodes, row_blocks * block), BF16),
        ),
        in_specs=[smem, smem, smem, whole((nodes // block, block)), whole(values.shape)],
        out_specs=(
            pl.BlockSpec((per_step * block, nodes), lambda i: (i, 0)),
            pl.BlockSpec((nodes, per_step * block), lambda i: (0, i)),
        ),
        scratch_shapes=[
            pltpu.VMEM((per_step * block, nodes), BF16),
            pltpu.VMEM((nodes, nodes), BF16),
        ],
        compiler_params=params(),
        cost_estimate=cost(4 * row_blocks * block * nodes * nodes, 2 * values.size),
        name="prep",
    )(rows, cols, count, order.reshape(nodes // block, block), values)


def product_kernel(pieces, *refs):
    matrix, parts, outs, joined = refs[0], refs[1 : 1 + pieces], refs[1 + pieces : -1], refs[-1]
    run = parts[0].shape[0]

    @pl.when(pl.program_id(0) == 0)
    def _():
        for i, part in enumerate(parts):
            joined[i * run : (i + 1) * run, :] = part[...]

    total = lax.dot_general(matrix[...], joined[...], (((1,), (0,)), ((), ())), preferred_element_type=F32)
    start = 0
    for out in outs:
        out[...] = total[start : start + out.shape[0]].astype(out.dtype)
        start += out.shape[0]


def product(matrix, parts, sizes, name):
    rows, depth = matrix.shape
    width = parts[0].shape[1]
    step = min(rows, 1024)
    if step == rows:
        out_shape = [jax.ShapeDtypeStruct((n, width), BF16) for n in sizes]
        out_specs = [whole((n, width)) for n in sizes]
    else:
        out_shape = [jax.ShapeDtypeStruct((rows, width), BF16)]
        out_specs = [pl.BlockSpec((step, width), lambda i: (i, 0))]
    outs = pl.pallas_call(
        functools.partial(product_kernel, len(parts)),
        grid=(rows // step,),
        out_shape=out_shape,
        in_specs=[pl.BlockSpec((step, depth), lambda i: (i, 0))] + [whole(p.shape) for p in parts],
        out_specs=out_specs,
        scratch_shapes=[pltpu.VMEM((depth, width), BF16)],
        compiler_params=params(),
        cost_estimate=cost(2 * rows * depth * width, 2 * (rows * depth + depth * width + rows * width)),
        name=name,
    )(matrix, *parts)
    if step == rows:
        return list(outs)
    cuts, start = [], 0
    for n in sizes:
        cuts.append(outs[0][start : start + n])
        start += n
    return cuts


def pointwise_kernel(terms, *refs):
    weight, bias, cotangent = refs[terms : terms + 3]
    activations, slopes, kept, sent, whole_term = refs[terms + 3 :]
    mixed = refs[0][...].astype(F32)
    for ref in refs[1:terms]:
        mixed = mixed + ref[...].astype(F32)
    high = mixed.astype(BF16)
    low = (mixed - high.astype(F32)).astype(BF16)
    preact = (
        jnp.dot(high, weight[...], preferred_element_type=F32)
        + jnp.dot(low, weight[...], preferred_element_type=F32)
        + bias[...]
    )
    gate = 1.0 / (1.0 + jnp.exp(-preact))
    activations[...] = (preact * gate).astype(BF16)
    slope = (cotangent[...].astype(F32) * (gate * (1.0 + preact * (1.0 - gate)))).astype(BF16)
    slopes[...] = slope
    whole_term[...] = lax.dot_general(high, slope, (((0,), (0,)), ((), ())), preferred_element_type=F32)
    half = kept.shape[0]
    core = lax.axis_index("col") & 1
    kept[...] = whole_term[pl.ds(pl.multiple_of(core * half, half), half), :].astype(kept.dtype)
    sent[...] = whole_term[pl.ds(pl.multiple_of((1 - core) * half, half), half), :].astype(sent.dtype)


def pointwise(terms, weight, bias, cotangent):
    nodes, width = cotangent.shape
    depth = weight.shape[0]
    node_out = jax.ShapeDtypeStruct((nodes, width), BF16)
    half_out = jax.ShapeDtypeStruct((depth // 2, width), BF16)
    return pl.pallas_call(
        functools.partial(pointwise_kernel, len(terms)),
        out_shape=(node_out, node_out, half_out, half_out),
        scratch_shapes=[pltpu.VMEM((depth, width), F32)],
        compiler_params=params(),
        cost_estimate=cost(6 * nodes * depth * width, 2 * nodes * width * (len(terms) + 5), nodes * width),
        name="pointwise",
    )(*terms, weight, bias.reshape(1, width), cotangent)


def feature_kernel(terms, *refs):
    total = refs[0][...].astype(F32)
    for ref in refs[1:terms]:
        total = total + ref[...].astype(F32)
    weight, out = refs[terms:]
    out[...] = lax.dot_general(total.astype(BF16), weight[...], NT, preferred_element_type=F32).astype(BF16)


def feature_gradient(terms, weight):
    nodes, width = terms[0].shape
    depth = weight.shape[0]
    return pl.pallas_call(
        functools.partial(feature_kernel, len(terms)),
        out_shape=jax.ShapeDtypeStruct((nodes, depth), BF16),
        compiler_params=params(),
        cost_estimate=cost(2 * nodes * depth * width, 2 * nodes * width * (len(terms) + 2)),
        name="feature_gradient",
    )(*terms, weight)


def add(left, right):
    return (left.astype(F32) + right.astype(F32)).astype(BF16)


def shards(
    features,
    weight,
    bias_term,
    block_values,
    block_rows,
    block_cols,
    counts,
    cluster_order,
    cotangent,
):
    node_count, width = features.shape
    row_devices = lax.axis_size("row")
    col_devices = lax.axis_size("col")
    levels = col_devices // 2
    values = block_values[0, 0]
    block = values.shape[1]
    row_blocks = node_count * col_devices // block

    with jax.named_scope("gather_features"):
        pieces = [features] + [swap(features, "row", m) for m in range(1, row_devices)]
    tile, tile_turned = prep(
        values, block_rows[0, 0], block_cols[0, 0], counts[0], cluster_order, row_blocks
    )

    with jax.named_scope("forward"):
        own = [node_count] * levels
        *kept, other = product(tile, pieces, own + [node_count * levels], "forward_tile")
        arrived = swap(other, "col", 1)
        pairs = [add(k, arrived[i * node_count : (i + 1) * node_count]) for i, k in enumerate(kept)]
        terms = [pairs[0]] + [swap(pairs[m], "col", 2 * m) for m in range(1, levels)]
        activations, slopes, weight_kept, weight_sent = pointwise(terms, weight, bias_term, cotangent)

    with jax.named_scope("gather_slopes"):
        slope_own = [slopes] + [swap(slopes, "col", 2 * m) for m in range(1, levels)]
    with jax.named_scope("weight_rows"):
        term = add(weight_kept, swap(weight_sent, "col", 1))
        mask = 1
        while mask < row_devices:
            term = add(term, swap(term, "row", mask))
            mask *= 2

    with jax.named_scope("backward"):
        slope_half = jnp.concatenate(slope_own)
        slope_other = swap(slope_half, "col", 1)
        node_terms = product(tile_turned, [slope_half, slope_other], [node_count] * row_devices, "backward_tile")
        node_sum = [node_terms[0]] + [swap(node_terms[m], "row", m) for m in range(1, row_devices)]
        grad_features = feature_gradient(node_sum, weight)

    with jax.named_scope("weight_levels"):
        mask = 2
        while mask < col_devices:
            term = add(term, swap(term, "col", mask))
            mask *= 2
        partner = swap(term, "col", 1)
        core = lax.axis_index("col") & 1
        scale = 1.0 / math.sqrt(node_count * row_devices * col_devices)
        both = jnp.where(
            core == 0, jnp.concatenate([term, partner]), jnp.concatenate([partner, term])
        )
        grad_weight = both.astype(F32) * scale
    return (activations, grad_features, grad_weight)


def solution(mesh):
    placed = (
        P(("col", "row"), None),
        P(),
        P(),
        P("row", "col", None, None, None),
        P("row", "col", None),
        P("row", "col", None),
        P("row", "col"),
        P("col"),
        P(("row", "col"), None),
    )
    return jax.shard_map(
        shards,
        mesh=mesh,
        in_specs=placed,
        out_specs=(P(("row", "col"), None), P(("col", "row"), None), P()),
        check_vma=False,
    )
```

```python
import functools
import math

import jax
import jax.numpy as jnp
from jax import lax
from jax.experimental import pallas as pl
from jax.experimental.pallas import tpu as pltpu
from jax.sharding import PartitionSpec as P

F32 = jnp.float32
BF16 = jnp.bfloat16
VMEM_LIMIT = 48 * 1024 * 1024


def params():
    return pltpu.CompilerParams(vmem_limit_bytes=VMEM_LIMIT)


def cost(flops, nbytes, transcendentals=0):
    return pl.CostEstimate(flops=flops, bytes_accessed=nbytes, transcendentals=transcendentals)


def whole(shape):
    return pl.BlockSpec(shape, lambda *_: (0,) * len(shape))


def swap(value, axis, mask):
    size = lax.axis_size(axis)
    return lax.ppermute(value, axis, [(i, i ^ mask) for i in range(size)])


def tiled_dot(shape, store, lhs_rows, rhs_rows):
    rows, cols = shape
    row_step, col_step = min(rows, 512), min(cols, 512)

    def tile(i, j):
        left = lhs_rows(pl.multiple_of(i * row_step, row_step), row_step)
        right = rhs_rows(pl.multiple_of(j * col_step, col_step), col_step)
        return lax.dot_general(left, right, NT, preferred_element_type=F32)

    def step(t, carry):
        i, j = t // (cols // col_step), t % (cols // col_step)
        value = tile(i, j)
        rows_at = pl.ds(pl.multiple_of(i * row_step, row_step), row_step)
        store(rows_at, pl.ds(pl.multiple_of(j * col_step, col_step), col_step), value)
        return carry

    steps = (rows // row_step) * (cols // col_step)
    if steps <= 4:
        for t in range(steps):
            step(t, 0)
    else:
        lax.fori_loop(0, steps, step, 0)


NT = (((1,), (1,)), ((), ()))


def prep_kernel(
    per_step, count, rows_hbm, cols_hbm, order_hbm, values_hbm, weight_hbm, bias_hbm, cotangent_hbm,
    a_ref, at_ref, weight_ref, bias_ref, cotangent_ref,
    dense, select, values, order, rows, cols, sems,
):
    block = values.shape[1]
    nodes = select.shape[0]
    first = pl.program_id(0) * per_step
    row_blocks = pl.num_programs(0) * per_step
    row, col = lax.axis_index("row"), lax.axis_index("col")
    pairs = (
        (order_hbm, order), (rows_hbm, rows), (cols_hbm, cols), (values_hbm, values),
        (weight_hbm, weight_ref), (bias_hbm, bias_ref), (cotangent_hbm, cotangent_ref),
    )
    copies = [pltpu.make_async_copy(src, dst, sems.at[i]) for i, (src, dst) in enumerate(pairs)]
    once = pl.program_id(0) == 0

    @pl.when(once)
    def _():
        for copy in copies:
            copy.start()

    dense[...] = jnp.zeros_like(dense)

    @pl.when(once)
    def _():
        copies[0].wait()
        local = lax.broadcasted_iota(jnp.int32, (block, block), 0)
        for chunk in range(nodes // block):
            node = (row ^ chunk) * block + local
            for part in range(nodes // block):
                hit = order[part : part + 1, :] == node
                select[chunk * block : (chunk + 1) * block, part * block : (part + 1) * block] = jnp.where(
                    hit, 1.0, 0.0
                ).astype(BF16)
        for copy in copies[1:]:
            copy.wait()

    def slot(s, carry):
        turned = rows[0, 0, s] ^ col
        place = (turned & 1) * (row_blocks // 2) + (turned >> 1) - first

        @pl.when((place >= 0) & (place < per_step))
        def _():
            dense[
                pl.ds(pl.multiple_of(place * block, block), block),
                pl.ds(pl.multiple_of(cols[0, 0, s] * block, block), block),
            ] = values[s]

        return carry

    lax.fori_loop(0, count[0, 0], slot, 0)

    def store_a(i, j, value):
        a_ref[i, j] = value.astype(BF16)

    def store_at(i, j, value):
        at_ref[i, j] = value.astype(BF16)

    dense_rows = lambda i, n: dense[pl.ds(i, n), :]
    select_rows = lambda i, n: select[pl.ds(i, n), :]
    tiled_dot((per_step * block, nodes), store_a, dense_rows, select_rows)
    tiled_dot((nodes, per_step * block), store_at, select_rows, dense_rows)


def prep(values, rows, cols, count, order, weight, bias, cotangent, row_blocks):
    capacity, block, _ = values.shape
    nodes = order.shape[0]
    per_step = min(row_blocks, 8)
    order = order.reshape(nodes // block, block)
    bias = bias.reshape(1, bias.shape[0])
    passed = (weight, bias, cotangent)
    return pl.pallas_call(
        functools.partial(prep_kernel, per_step),
        grid=(row_blocks // per_step,),
        out_shape=(
            jax.ShapeDtypeStruct((row_blocks * block, nodes), BF16),
            jax.ShapeDtypeStruct((nodes, row_blocks * block), BF16),
        )
        + tuple(jax.ShapeDtypeStruct(p.shape, p.dtype) for p in passed),
        in_specs=[pl.BlockSpec(memory_space=pltpu.SMEM)] + [pl.BlockSpec(memory_space=pltpu.HBM)] * 7,
        out_specs=(
            pl.BlockSpec((per_step * block, nodes), lambda i: (i, 0)),
            pl.BlockSpec((nodes, per_step * block), lambda i: (0, i)),
        )
        + tuple(whole(p.shape) for p in passed),
        scratch_shapes=[
            pltpu.VMEM((per_step * block, nodes), BF16),
            pltpu.VMEM((nodes, nodes), BF16),
            pltpu.VMEM(values.shape, BF16),
            pltpu.VMEM(order.shape, jnp.int32),
            pltpu.SMEM(rows.shape, jnp.int32),
            pltpu.SMEM(cols.shape, jnp.int32),
            pltpu.SemaphoreType.DMA((7,)),
        ],
        compiler_params=params(),
        cost_estimate=cost(4 * row_blocks * block * nodes * nodes, 2 * values.size),
        name="prep",
    )(count, *(pltpu.with_memory_space_constraint(x, pltpu.HBM) for x in (rows, cols, order, values, *passed)))


def product_kernel(pieces, *refs):
    matrix, parts, outs, joined = refs[0], refs[1 : 1 + pieces], refs[1 + pieces : -1], refs[-1]
    run = parts[0].shape[0]

    @pl.when(pl.program_id(0) == 0)
    def _():
        for i, part in enumerate(parts):
            joined[i * run : (i + 1) * run, :] = part[...]

    total = lax.dot_general(matrix[...], joined[...], (((1,), (0,)), ((), ())), preferred_element_type=F32)
    start = 0
    for out in outs:
        out[...] = total[start : start + out.shape[0]].astype(out.dtype)
        start += out.shape[0]


def product(matrix, parts, sizes, name):
    rows, depth = matrix.shape
    width = parts[0].shape[1]
    step = min(rows, 1024)
    if step == rows:
        out_shape = [jax.ShapeDtypeStruct((n, width), BF16) for n in sizes]
        out_specs = [whole((n, width)) for n in sizes]
    else:
        out_shape = [jax.ShapeDtypeStruct((rows, width), BF16)]
        out_specs = [pl.BlockSpec((step, width), lambda i: (i, 0))]
    outs = pl.pallas_call(
        functools.partial(product_kernel, len(parts)),
        grid=(rows // step,),
        out_shape=out_shape,
        in_specs=[pl.BlockSpec((step, depth), lambda i: (i, 0))] + [whole(p.shape) for p in parts],
        out_specs=out_specs,
        scratch_shapes=[pltpu.VMEM((depth, width), BF16)],
        compiler_params=params(),
        cost_estimate=cost(2 * rows * depth * width, 2 * (rows * depth + depth * width + rows * width)),
        name=name,
    )(matrix, *parts)
    if step == rows:
        return list(outs)
    cuts, start = [], 0
    for n in sizes:
        cuts.append(outs[0][start : start + n])
        start += n
    return cuts


def slopes_kernel(terms, *refs):
    weight, bias, cotangent = refs[terms : terms + 3]
    preact_ref, slopes, kept, sent, whole_term = refs[terms + 3 :]
    mixed = refs[0][...].astype(F32)
    for ref in refs[1:terms]:
        mixed = mixed + ref[...].astype(F32)
    high = mixed.astype(BF16)
    low = (mixed - high.astype(F32)).astype(BF16)
    preact = (
        jnp.dot(high, weight[...], preferred_element_type=F32)
        + jnp.dot(low, weight[...], preferred_element_type=F32)
        + bias[...]
    )
    preact_ref[...] = preact
    gate = 1.0 / (1.0 + jnp.exp(-preact))
    slope = (cotangent[...].astype(F32) * (gate * (1.0 + preact * (1.0 - gate)))).astype(BF16)
    slopes[...] = slope
    whole_term[...] = lax.dot_general(high, slope, (((0,), (0,)), ((), ())), preferred_element_type=F32)
    half = kept.shape[0]
    core = lax.axis_index("col") & 1
    kept[...] = whole_term[pl.ds(pl.multiple_of(core * half, half), half), :].astype(kept.dtype)
    sent[...] = whole_term[pl.ds(pl.multiple_of((1 - core) * half, half), half), :].astype(sent.dtype)


def slopes_of(terms, weight, bias, cotangent):
    nodes, width = cotangent.shape
    depth = weight.shape[0]
    half_out = jax.ShapeDtypeStruct((depth // 2, width), BF16)
    return pl.pallas_call(
        functools.partial(slopes_kernel, len(terms)),
        out_shape=(
            jax.ShapeDtypeStruct((nodes, width), F32),
            jax.ShapeDtypeStruct((nodes, width), BF16),
            half_out,
            half_out,
        ),
        scratch_shapes=[pltpu.VMEM((depth, width), F32)],
        compiler_params=params(),
        cost_estimate=cost(6 * nodes * depth * width, 2 * nodes * width * (len(terms) + 5), nodes * width),
        name="slopes",
    )(*terms, weight, bias, cotangent)


def activation_kernel(preact_ref, out):
    preact = preact_ref[...]
    out[...] = (preact / (1.0 + jnp.exp(-preact))).astype(BF16)


def activation(preact):
    return pl.pallas_call(
        activation_kernel,
        out_shape=jax.ShapeDtypeStruct(preact.shape, BF16),
        compiler_params=params(),
        cost_estimate=cost(4 * preact.size, 6 * preact.size, preact.size),
        name="activation",
    )(preact)


def feature_kernel(terms, *refs):
    total = refs[0][...].astype(F32)
    for ref in refs[1:terms]:
        total = total + ref[...].astype(F32)
    weight, out = refs[terms:]
    out[...] = lax.dot_general(total.astype(BF16), weight[...], NT, preferred_element_type=F32).astype(BF16)


def feature_gradient(terms, weight):
    nodes, width = terms[0].shape
    depth = weight.shape[0]
    return pl.pallas_call(
        functools.partial(feature_kernel, len(terms)),
        out_shape=jax.ShapeDtypeStruct((nodes, depth), BF16),
        compiler_params=params(),
        cost_estimate=cost(2 * nodes * depth * width, 2 * nodes * width * (len(terms) + 2)),
        name="feature_gradient",
    )(*terms, weight)


def add(left, right):
    return (left.astype(F32) + right.astype(F32)).astype(BF16)


def shards(
    features,
    weight,
    bias_term,
    block_values,
    block_rows,
    block_cols,
    counts,
    cluster_order,
    cotangent,
):
    node_count, width = features.shape
    row_devices = lax.axis_size("row")
    col_devices = lax.axis_size("col")
    levels = col_devices // 2
    block = block_values.shape[3]
    row_blocks = node_count * col_devices // block

    with jax.named_scope("gather_features"):
        pieces = [features] + [swap(features, "row", m) for m in range(1, row_devices)]
    tile, tile_turned, weight_near, bias_near, cotangent_near = prep(
        block_values[0, 0], block_rows, block_cols, counts, cluster_order, weight, bias_term, cotangent, row_blocks
    )

    with jax.named_scope("forward"):
        own = [node_count] * levels
        *kept, other = product(tile, pieces, own + [node_count * levels], "forward_tile")
        arrived = swap(other, "col", 1)
        pairs = [add(k, arrived[i * node_count : (i + 1) * node_count]) for i, k in enumerate(kept)]
        terms = [pairs[0]] + [swap(pairs[m], "col", 2 * m) for m in range(1, levels)]
        preact, slopes, weight_kept, weight_sent = slopes_of(terms, weight_near, bias_near, cotangent_near)

    with jax.named_scope("gather_slopes"):
        slope_own = [slopes] + [swap(slopes, "col", 2 * m) for m in range(1, levels)]
    activations = activation(preact)

    with jax.named_scope("weight_rows"):
        term = add(weight_kept, swap(weight_sent, "col", 1))
        masks = [1 << i for i in range((row_devices - 1).bit_length())]
        for mask in masks[:-1]:
            term = add(term, swap(term, "row", mask))
        last = swap(term, "row", masks[-1])

    with jax.named_scope("backward"):
        slope_half = jnp.concatenate(slope_own)
        slope_half, last = lax.optimization_barrier((slope_half, last))
        slope_other = swap(slope_half, "col", 1)
        node_terms = product(
            tile_turned, [slope_half, slope_other], [node_count] * row_devices, "backward_tile"
        )

    with jax.named_scope("weight_levels"):
        term = add(term, last)
        masks = [2 << i for i in range((levels - 1).bit_length())]
        for mask in masks[:-1]:
            other = swap(term, "col", mask)
            if mask == 2:
                other, node_terms[0] = lax.optimization_barrier((other, node_terms[0]))
            term = add(term, other)
        last = swap(term, "col", masks[-1])

    with jax.named_scope("backward"):
        node_sum = [node_terms[0]] + [swap(node_terms[m], "row", m) for m in range(1, row_devices)]
        grad_features = feature_gradient(node_sum, weight_near)

    with jax.named_scope("weight_levels"):
        term = add(term, last)
        partner = swap(term, "col", 1)
        core = lax.axis_index("col") & 1
        scale = 1.0 / math.sqrt(node_count * row_devices * col_devices)
        both = jnp.where(
            core == 0, jnp.concatenate([term, partner]), jnp.concatenate([partner, term])
        )
        grad_weight = both.astype(F32) * scale
    return (activations, grad_features, grad_weight)


def solution(mesh):
    placed = (
        P(("col", "row"), None),
        P(),
        P(),
        P("row", "col", None, None, None),
        P("row", "col", None),
        P("row", "col", None),
        P("row", "col"),
        P("col"),
        P(("row", "col"), None),
    )
    return jax.shard_map(
        shards,
        mesh=mesh,
        in_specs=placed,
        out_specs=(P(("row", "col"), None), P(("col", "row"), None), P()),
        check_vma=False,
    )
```

```python
import functools
import math

import jax
import jax.numpy as jnp
from jax import lax
from jax.experimental import pallas as pl
from jax.experimental.pallas import tpu as pltpu
from jax.sharding import PartitionSpec as P

F32 = jnp.float32
BF16 = jnp.bfloat16
MIB = 1024 * 1024


def params(tile_bytes=0):
    return pltpu.CompilerParams(vmem_limit_bytes=(8 if tile_bytes <= MIB else 48) * MIB)


def cost(flops, nbytes, transcendentals=0):
    return pl.CostEstimate(flops=flops, bytes_accessed=nbytes, transcendentals=transcendentals)


def whole(shape):
    return pl.BlockSpec(shape, lambda *_: (0,) * len(shape))


def swap(value, axis, mask):
    size = lax.axis_size(axis)
    return lax.ppermute(value, axis, [(i, i ^ mask) for i in range(size)])


def exchange(values, axis, unit):
    out = list(values)
    for m in reversed(range(1, len(values))):
        out[m] = swap(values[m], axis, m * unit)
    return out


def far_first(count):
    return list(reversed(range(count)))


def ordered(values, order):
    return [values[i] for i in order]


def runs_of(order, size):
    return [(order.index(i), 0, size) for i in range(len(order))]


def tiled_dot(shape, store, lhs_rows, rhs_rows):
    rows, cols = shape
    row_step, col_step = min(rows, 512), min(cols, 512)

    def tile(i, j):
        left = lhs_rows(pl.multiple_of(i * row_step, row_step), row_step)
        right = rhs_rows(pl.multiple_of(j * col_step, col_step), col_step)
        return lax.dot_general(left, right, NT, preferred_element_type=F32)

    def step(t, carry):
        i, j = t // (cols // col_step), t % (cols // col_step)
        value = tile(i, j)
        rows_at = pl.ds(pl.multiple_of(i * row_step, row_step), row_step)
        store(rows_at, pl.ds(pl.multiple_of(j * col_step, col_step), col_step), value)
        return carry

    steps = (rows // row_step) * (cols // col_step)
    if steps <= 4:
        for t in range(steps):
            step(t, 0)
    else:
        lax.fori_loop(0, steps, step, 0)


NT = (((1,), (1,)), ((), ()))


def prep_kernel(
    per_step, count, rows_hbm, cols_hbm, order_hbm, values_hbm, weight_hbm, bias_hbm, cotangent_hbm,
    a_ref, at_ref, weight_ref, bias_ref, cotangent_ref,
    dense, select, values, order, rows, cols, sems,
):
    block = values.shape[1]
    nodes = select.shape[0]
    first = pl.program_id(0) * per_step
    row_blocks = pl.num_programs(0) * per_step
    row, col = lax.axis_index("row"), lax.axis_index("col")
    pairs = (
        (order_hbm, order), (rows_hbm, rows), (cols_hbm, cols), (values_hbm, values),
        (weight_hbm, weight_ref), (bias_hbm, bias_ref), (cotangent_hbm, cotangent_ref),
    )
    copies = [pltpu.make_async_copy(src, dst, sems.at[i]) for i, (src, dst) in enumerate(pairs)]
    once = pl.program_id(0) == 0

    @pl.when(once)
    def _():
        for copy in copies:
            copy.start()

    dense[...] = jnp.zeros_like(dense)

    @pl.when(once)
    def _():
        copies[0].wait()
        local = lax.broadcasted_iota(jnp.int32, (block, block), 0)
        for chunk in range(nodes // block):
            node = (row ^ chunk) * block + local
            for part in range(nodes // block):
                hit = order[part : part + 1, :] == node
                select[chunk * block : (chunk + 1) * block, part * block : (part + 1) * block] = jnp.where(
                    hit, 1.0, 0.0
                ).astype(BF16)
        for copy in copies[1:]:
            copy.wait()

    def slot(s, carry):
        turned = rows[0, 0, s] ^ col
        place = (turned & 1) * (row_blocks // 2) + (turned >> 1) - first

        @pl.when((place >= 0) & (place < per_step))
        def _():
            dense[
                pl.ds(pl.multiple_of(place * block, block), block),
                pl.ds(pl.multiple_of(cols[0, 0, s] * block, block), block),
            ] = values[s]

        return carry

    lax.fori_loop(0, count[0, 0], slot, 0)

    def store_a(i, j, value):
        a_ref[i, j] = value.astype(BF16)

    def store_at(i, j, value):
        at_ref[i, j] = value.astype(BF16)

    dense_rows = lambda i, n: dense[pl.ds(i, n), :]
    select_rows = lambda i, n: select[pl.ds(i, n), :]
    tiled_dot((per_step * block, nodes), store_a, dense_rows, select_rows)
    tiled_dot((nodes, per_step * block), store_at, select_rows, dense_rows)


def prep(values, rows, cols, count, order, weight, bias, cotangent, row_blocks):
    capacity, block, _ = values.shape
    nodes = order.shape[0]
    per_step = min(row_blocks, 8)
    order = order.reshape(nodes // block, block)
    bias = bias.reshape(1, bias.shape[0])
    passed = (weight, bias, cotangent)
    return pl.pallas_call(
        functools.partial(prep_kernel, per_step),
        grid=(row_blocks // per_step,),
        out_shape=(
            jax.ShapeDtypeStruct((row_blocks * block, nodes), BF16),
            jax.ShapeDtypeStruct((nodes, row_blocks * block), BF16),
        )
        + tuple(jax.ShapeDtypeStruct(p.shape, p.dtype) for p in passed),
        in_specs=[pl.BlockSpec(memory_space=pltpu.SMEM)] + [pl.BlockSpec(memory_space=pltpu.HBM)] * 7,
        out_specs=(
            pl.BlockSpec((per_step * block, nodes), lambda i: (i, 0)),
            pl.BlockSpec((nodes, per_step * block), lambda i: (0, i)),
        )
        + tuple(whole(p.shape) for p in passed),
        scratch_shapes=[
            pltpu.VMEM((per_step * block, nodes), BF16),
            pltpu.VMEM((nodes, nodes), BF16),
            pltpu.VMEM(values.shape, BF16),
            pltpu.VMEM(order.shape, jnp.int32),
            pltpu.SMEM(rows.shape, jnp.int32),
            pltpu.SMEM(cols.shape, jnp.int32),
            pltpu.SemaphoreType.DMA((7,)),
        ],
        compiler_params=params(2 * row_blocks * block * nodes),
        cost_estimate=cost(4 * row_blocks * block * nodes * nodes, 2 * values.size),
        name="prep",
    )(count, *(pltpu.with_memory_space_constraint(x, pltpu.HBM) for x in (rows, cols, order, values, *passed)))


def product_kernel(count, runs, *refs):
    matrix, parts, outs, joined = refs[0], refs[1 : 1 + count], refs[1 + count : -1], refs[-1]

    @pl.when(pl.program_id(0) == 0)
    def _():
        start = 0
        for part, first, size in runs:
            joined[start : start + size, :] = parts[part][first : first + size, :]
            start += size

    total = lax.dot_general(matrix[...], joined[...], (((1,), (0,)), ((), ())), preferred_element_type=F32)
    start = 0
    for out in outs:
        out[...] = total[start : start + out.shape[0]].astype(out.dtype)
        start += out.shape[0]


def product(matrix, parts, runs, sizes, name):
    rows, depth = matrix.shape
    width = parts[0].shape[1]
    step = min(rows, 1024)
    if step == rows:
        out_shape = [jax.ShapeDtypeStruct((n, width), BF16) for n in sizes]
        out_specs = [whole((n, width)) for n in sizes]
    else:
        out_shape = [jax.ShapeDtypeStruct((rows, width), BF16)]
        out_specs = [pl.BlockSpec((step, width), lambda i: (i, 0))]
    outs = pl.pallas_call(
        functools.partial(product_kernel, len(parts), tuple(runs)),
        grid=(rows // step,),
        out_shape=out_shape,
        in_specs=[pl.BlockSpec((step, depth), lambda i: (i, 0))] + [whole(p.shape) for p in parts],
        out_specs=out_specs,
        scratch_shapes=[pltpu.VMEM((depth, width), BF16)],
        compiler_params=params(2 * rows * depth),
        cost_estimate=cost(2 * rows * depth * width, 2 * (rows * depth + depth * width + rows * width)),
        name=name,
    )(matrix, *parts)
    if step == rows:
        return list(outs)
    cuts, start = [], 0
    for n in sizes:
        cuts.append(outs[0][start : start + n])
        start += n
    return cuts


def slopes_kernel(terms, *refs):
    weight, bias, cotangent = refs[terms : terms + 3]
    preact_ref, slopes, kept, sent, whole_term = refs[terms + 3 :]
    mixed = refs[0][...].astype(F32)
    for ref in refs[1:terms]:
        mixed = mixed + ref[...].astype(F32)
    high = mixed.astype(BF16)
    low = (mixed - high.astype(F32)).astype(BF16)
    preact = (
        jnp.dot(high, weight[...], preferred_element_type=F32)
        + jnp.dot(low, weight[...], preferred_element_type=F32)
        + bias[...]
    )
    preact_ref[...] = preact
    gate = 1.0 / (1.0 + jnp.exp(-preact))
    slope = (cotangent[...].astype(F32) * (gate * (1.0 + preact * (1.0 - gate)))).astype(BF16)
    slopes[...] = slope
    whole_term[...] = lax.dot_general(high, slope, (((0,), (0,)), ((), ())), preferred_element_type=F32)
    half = kept.shape[0]
    core = lax.axis_index("col") & 1
    kept[...] = whole_term[pl.ds(pl.multiple_of(core * half, half), half), :].astype(kept.dtype)
    sent[...] = whole_term[pl.ds(pl.multiple_of((1 - core) * half, half), half), :].astype(sent.dtype)


def slopes_of(terms, weight, bias, cotangent):
    nodes, width = cotangent.shape
    depth = weight.shape[0]
    half_out = jax.ShapeDtypeStruct((depth // 2, width), BF16)
    return pl.pallas_call(
        functools.partial(slopes_kernel, len(terms)),
        out_shape=(
            jax.ShapeDtypeStruct((nodes, width), F32),
            jax.ShapeDtypeStruct((nodes, width), BF16),
            half_out,
            half_out,
        ),
        scratch_shapes=[pltpu.VMEM((depth, width), F32)],
        compiler_params=params(),
        cost_estimate=cost(6 * nodes * depth * width, 2 * nodes * width * (len(terms) + 5), nodes * width),
        name="slopes",
    )(*terms, weight, bias, cotangent)


def activation_kernel(preact_ref, out):
    preact = preact_ref[...]
    out[...] = (preact / (1.0 + jnp.exp(-preact))).astype(BF16)


def activation(preact):
    return pl.pallas_call(
        activation_kernel,
        out_shape=jax.ShapeDtypeStruct(preact.shape, BF16),
        compiler_params=params(),
        cost_estimate=cost(4 * preact.size, 6 * preact.size, preact.size),
        name="activation",
    )(preact)


def feature_kernel(terms, *refs):
    weight, out = refs[terms:]
    nodes = out.shape[0]
    total = refs[0][...].astype(F32)
    for ref in refs[1:terms]:
        total = total + ref[:nodes, :].astype(F32)
    out[...] = lax.dot_general(total.astype(BF16), weight[...], NT, preferred_element_type=F32).astype(BF16)


def feature_gradient(terms, weight):
    nodes, width = terms[0].shape
    depth = weight.shape[0]
    return pl.pallas_call(
        functools.partial(feature_kernel, len(terms)),
        out_shape=jax.ShapeDtypeStruct((nodes, depth), BF16),
        compiler_params=params(),
        cost_estimate=cost(2 * nodes * depth * width, 2 * nodes * width * (len(terms) + 2)),
        name="feature_gradient",
    )(*terms, weight)


def add(left, right):
    return (left.astype(F32) + right.astype(F32)).astype(BF16)


def shards(
    features,
    weight,
    bias_term,
    block_values,
    block_rows,
    block_cols,
    counts,
    cluster_order,
    cotangent,
):
    node_count, width = features.shape
    row_devices = lax.axis_size("row")
    col_devices = lax.axis_size("col")
    levels = col_devices // 2
    block = block_values.shape[3]
    row_blocks = node_count * col_devices // block

    row_masks = [1 << i for i in range((row_devices - 1).bit_length())]
    level_masks = [2 << i for i in reversed(range((levels - 1).bit_length()))]
    row_order, level_order = far_first(row_devices), far_first(levels)
    with jax.named_scope("gather_features"):
        pieces = exchange([features] * row_devices, "row", 1)
    tile, tile_turned, weight_near, bias_near, cotangent_near = prep(
        block_values[0, 0], block_rows, block_cols, counts, cluster_order, weight, bias_term, cotangent, row_blocks
    )

    with jax.named_scope("forward"):
        *kept, other = product(
            tile,
            ordered(pieces, row_order),
            runs_of(row_order, node_count),
            [node_count] * levels + [node_count * levels],
            "forward_tile",
        )
        arrived = swap(other, "col", 1)
        pairs = [add(k, arrived[i * node_count : (i + 1) * node_count]) for i, k in enumerate(kept)]
        terms = exchange(pairs, "col", 2)
        preact, slopes, weight_kept, weight_sent = slopes_of(
            ordered(terms, level_order), weight_near, bias_near, cotangent_near
        )
    activations = activation(preact)

    with jax.named_scope("gather_slopes"):
        slope_own = exchange([slopes] * levels, "col", 2)

    with jax.named_scope("weight_rows"):
        term = add(weight_kept, swap(weight_sent, "col", 1))
        for mask in row_masks:
            other = swap(term, "row", mask)
            if mask == row_masks[-1]:
                other, _ = lax.optimization_barrier((other, slope_own[1:]))
            term = add(term, other)

    with jax.named_scope("backward"):
        far = ordered(slope_own, level_order)
        slope_other = swap(jnp.concatenate(far), "col", 1)
        runs = runs_of(level_order, node_count)
        node_terms = product(
            tile_turned,
            far + [slope_other],
            runs + [(levels, part * node_count, node_count) for part, _, _ in runs],
            [node_count] * row_devices,
            "backward_tile",
        )
        node_sum = exchange(node_terms, "row", 1)
        grad_features = feature_gradient(ordered(node_sum, row_order), weight_near)

    with jax.named_scope("weight_levels"):
        for mask in level_masks:
            other = swap(term, "col", mask)
            if mask == level_masks[-1]:
                other, _ = lax.optimization_barrier((other, grad_features))
            term = add(term, other)
        partner = swap(term, "col", 1)
        core = lax.axis_index("col") & 1
        scale = 1.0 / math.sqrt(node_count * row_devices * col_devices)
        both = jnp.where(
            core == 0, jnp.concatenate([term, partner]), jnp.concatenate([partner, term])
        )
        grad_weight = both.astype(F32) * scale
    return (activations, grad_features, grad_weight)


def solution(mesh):
    placed = (
        P(("col", "row"), None),
        P(),
        P(),
        P("row", "col", None, None, None),
        P("row", "col", None),
        P("row", "col", None),
        P("row", "col"),
        P("col"),
        P(("row", "col"), None),
    )
    return jax.shard_map(
        shards,
        mesh=mesh,
        in_specs=placed,
        out_specs=(P(("row", "col"), None), P(("col", "row"), None), P()),
        check_vma=False,
    )
```

```python
import functools
import math

import jax
import jax.numpy as jnp
from jax import lax
from jax.experimental import pallas as pl
from jax.experimental.pallas import tpu as pltpu
from jax.sharding import PartitionSpec as P

F32 = jnp.float32
BF16 = jnp.bfloat16
MIB = 1024 * 1024


def params(tile_bytes=0):
    return pltpu.CompilerParams(vmem_limit_bytes=(8 if tile_bytes <= MIB else 48) * MIB)


def cost(flops, nbytes, transcendentals=0):
    return pl.CostEstimate(flops=flops, bytes_accessed=nbytes, transcendentals=transcendentals)


def whole(shape):
    return pl.BlockSpec(shape, lambda *_: (0,) * len(shape))


def swap(value, axis, mask):
    size = lax.axis_size(axis)
    return lax.ppermute(value, axis, [(i, i ^ mask) for i in range(size)])


def exchange(values, axis, unit):
    out = list(values)
    for m in reversed(range(1, len(values))):
        out[m] = swap(values[m], axis, m * unit)
    return out


def far_first(count):
    return list(reversed(range(count)))


def ordered(values, order):
    return [values[i] for i in order]


def runs_of(order, size):
    return [(order.index(i), 0, size) for i in range(len(order))]


def tiled_dot(shape, store, lhs_rows, rhs_rows):
    rows, cols = shape
    row_step, col_step = min(rows, 512), min(cols, 512)

    def tile(i, j):
        left = lhs_rows(pl.multiple_of(i * row_step, row_step), row_step)
        right = rhs_rows(pl.multiple_of(j * col_step, col_step), col_step)
        return lax.dot_general(left, right, NT, preferred_element_type=F32)

    def step(t, carry):
        i, j = t // (cols // col_step), t % (cols // col_step)
        value = tile(i, j)
        rows_at = pl.ds(pl.multiple_of(i * row_step, row_step), row_step)
        store(rows_at, pl.ds(pl.multiple_of(j * col_step, col_step), col_step), value)
        return carry

    steps = (rows // row_step) * (cols // col_step)
    if steps <= 4:
        for t in range(steps):
            step(t, 0)
    else:
        lax.fori_loop(0, steps, step, 0)


NT = (((1,), (1,)), ((), ()))


def prep_kernel(
    per_step, count, rows_hbm, cols_hbm, order_hbm, values_hbm, weight_hbm, bias_hbm, cotangent_hbm,
    a_ref, at_ref, weight_ref, bias_ref, cotangent_ref,
    dense, select, values, order, rows, cols, sems,
):
    block = values.shape[1]
    nodes = select.shape[0]
    first = pl.program_id(0) * per_step
    row_blocks = pl.num_programs(0) * per_step
    row, col = lax.axis_index("row"), lax.axis_index("col")
    pairs = (
        (order_hbm, order), (rows_hbm, rows), (cols_hbm, cols), (values_hbm, values),
        (weight_hbm, weight_ref), (bias_hbm, bias_ref), (cotangent_hbm, cotangent_ref),
    )
    copies = [pltpu.make_async_copy(src, dst, sems.at[i]) for i, (src, dst) in enumerate(pairs)]
    once = pl.program_id(0) == 0

    @pl.when(once)
    def _():
        for copy in copies:
            copy.start()

    dense[...] = jnp.zeros_like(dense)

    @pl.when(once)
    def _():
        copies[0].wait()
        local = lax.broadcasted_iota(jnp.int32, (block, block), 0)
        for chunk in range(nodes // block):
            node = (row ^ chunk) * block + local
            for part in range(nodes // block):
                hit = order[part : part + 1, :] == node
                select[chunk * block : (chunk + 1) * block, part * block : (part + 1) * block] = jnp.where(
                    hit, 1.0, 0.0
                ).astype(BF16)
        for copy in copies[1:]:
            copy.wait()

    def slot(s, carry):
        turned = rows[0, 0, s] ^ col
        place = (turned & 1) * (row_blocks // 2) + (turned >> 1) - first

        @pl.when((place >= 0) & (place < per_step))
        def _():
            dense[
                pl.ds(pl.multiple_of(place * block, block), block),
                pl.ds(pl.multiple_of(cols[0, 0, s] * block, block), block),
            ] = values[s]

        return carry

    lax.fori_loop(0, count[0, 0], slot, 0)

    def store_a(i, j, value):
        a_ref[i, j] = value.astype(BF16)

    def store_at(i, j, value):
        at_ref[i, j] = value.astype(BF16)

    dense_rows = lambda i, n: dense[pl.ds(i, n), :]
    select_rows = lambda i, n: select[pl.ds(i, n), :]
    tiled_dot((per_step * block, nodes), store_a, dense_rows, select_rows)
    tiled_dot((nodes, per_step * block), store_at, select_rows, dense_rows)


def prep(values, rows, cols, count, order, weight, bias, cotangent, row_blocks):
    capacity, block, _ = values.shape
    nodes = order.shape[0]
    per_step = min(row_blocks, 8)
    order = order.reshape(nodes // block, block)
    bias = bias.reshape(1, bias.shape[0])
    passed = (weight, bias, cotangent)
    return pl.pallas_call(
        functools.partial(prep_kernel, per_step),
        grid=(row_blocks // per_step,),
        out_shape=(
            jax.ShapeDtypeStruct((row_blocks * block, nodes), BF16),
            jax.ShapeDtypeStruct((nodes, row_blocks * block), BF16),
        )
        + tuple(jax.ShapeDtypeStruct(p.shape, p.dtype) for p in passed),
        in_specs=[pl.BlockSpec(memory_space=pltpu.SMEM)] + [pl.BlockSpec(memory_space=pltpu.HBM)] * 7,
        out_specs=(
            pl.BlockSpec((per_step * block, nodes), lambda i: (i, 0)),
            pl.BlockSpec((nodes, per_step * block), lambda i: (0, i)),
        )
        + tuple(whole(p.shape) for p in passed),
        scratch_shapes=[
            pltpu.VMEM((per_step * block, nodes), BF16),
            pltpu.VMEM((nodes, nodes), BF16),
            pltpu.VMEM(values.shape, BF16),
            pltpu.VMEM(order.shape, jnp.int32),
            pltpu.SMEM(rows.shape, jnp.int32),
            pltpu.SMEM(cols.shape, jnp.int32),
            pltpu.SemaphoreType.DMA((7,)),
        ],
        compiler_params=params(2 * row_blocks * block * nodes),
        cost_estimate=cost(4 * row_blocks * block * nodes * nodes, 2 * values.size),
        name="prep",
    )(count, *(pltpu.with_memory_space_constraint(x, pltpu.HBM) for x in (rows, cols, order, values, *passed)))


def product_kernel(count, runs, top, *refs):
    matrix, parts, outs, joined = refs[0], refs[1 : 1 + count], refs[1 + count : -1], refs[-1]

    @pl.when(pl.program_id(0) == 0)
    def _():
        start = 0
        for part, first, size in runs:
            joined[start : start + size, :] = parts[part][first : first + size, :]
            start += size

    rows = sum(out.shape[0] for out in outs)
    total = lax.dot_general(
        matrix[top : top + rows, :], joined[...], (((1,), (0,)), ((), ())), preferred_element_type=F32
    )
    start = 0
    for out in outs:
        out[...] = total[start : start + out.shape[0]].astype(out.dtype)
        start += out.shape[0]


def product(matrix, parts, runs, sizes, name, top=0):
    rows, depth = sum(sizes), matrix.shape[1]
    width = parts[0].shape[1]
    small = matrix.size <= MIB
    if small:
        step = rows
        matrix_spec = whole(matrix.shape)
        out_shape = [jax.ShapeDtypeStruct((n, width), BF16) for n in sizes]
        out_specs = [whole((n, width)) for n in sizes]
    else:
        step = math.gcd(math.gcd(rows, top), 1024)
        matrix_spec = pl.BlockSpec((step, depth), lambda i: (top // step + i, 0))
        out_shape = [jax.ShapeDtypeStruct((rows, width), BF16)]
        out_specs = [pl.BlockSpec((step, width), lambda i: (i, 0))]
    outs = pl.pallas_call(
        functools.partial(product_kernel, len(parts), tuple(runs), top if small else 0),
        grid=(rows // step,),
        out_shape=out_shape,
        in_specs=[matrix_spec] + [whole(p.shape) for p in parts],
        out_specs=out_specs,
        scratch_shapes=[pltpu.VMEM((depth, width), BF16)],
        compiler_params=params(2 * matrix.size),
        cost_estimate=cost(2 * rows * depth * width, 2 * (rows * depth + depth * width + rows * width)),
        name=name,
    )(matrix, *parts)
    if small:
        return list(outs)
    cuts, start = [], 0
    for n in sizes:
        cuts.append(outs[0][start : start + n])
        start += n
    return cuts


def slopes_kernel(terms, *refs):
    weight, bias, cotangent = refs[terms : terms + 3]
    preact_ref, slopes, kept, sent, whole_term = refs[terms + 3 :]
    mixed = refs[0][...].astype(F32)
    for ref in refs[1:terms]:
        mixed = mixed + ref[...].astype(F32)
    high = mixed.astype(BF16)
    low = (mixed - high.astype(F32)).astype(BF16)
    preact = (
        jnp.dot(high, weight[...], preferred_element_type=F32)
        + jnp.dot(low, weight[...], preferred_element_type=F32)
        + bias[...]
    )
    preact_ref[...] = preact
    gate = 1.0 / (1.0 + jnp.exp(-preact))
    slope = (cotangent[...].astype(F32) * (gate * (1.0 + preact * (1.0 - gate)))).astype(BF16)
    slopes[...] = slope
    whole_term[...] = lax.dot_general(high, slope, (((0,), (0,)), ((), ())), preferred_element_type=F32)
    half = kept.shape[0]
    core = lax.axis_index("col") & 1
    kept[...] = whole_term[pl.ds(pl.multiple_of(core * half, half), half), :].astype(kept.dtype)
    sent[...] = whole_term[pl.ds(pl.multiple_of((1 - core) * half, half), half), :].astype(sent.dtype)


def slopes_of(terms, weight, bias, cotangent):
    nodes, width = cotangent.shape
    depth = weight.shape[0]
    half_out = jax.ShapeDtypeStruct((depth // 2, width), BF16)
    return pl.pallas_call(
        functools.partial(slopes_kernel, len(terms)),
        out_shape=(
            jax.ShapeDtypeStruct((nodes, width), F32),
            jax.ShapeDtypeStruct((nodes, width), BF16),
            half_out,
            half_out,
        ),
        scratch_shapes=[pltpu.VMEM((depth, width), F32)],
        compiler_params=params(),
        cost_estimate=cost(6 * nodes * depth * width, 2 * nodes * width * (len(terms) + 5), nodes * width),
        name="slopes",
    )(*terms, weight, bias, cotangent)


def activation_kernel(preact_ref, out):
    preact = preact_ref[...]
    out[...] = (preact / (1.0 + jnp.exp(-preact))).astype(BF16)


def activation(preact):
    return pl.pallas_call(
        activation_kernel,
        out_shape=jax.ShapeDtypeStruct(preact.shape, BF16),
        compiler_params=params(),
        cost_estimate=cost(4 * preact.size, 6 * preact.size, preact.size),
        name="activation",
    )(preact)


def feature_kernel(terms, *refs):
    weight, out = refs[terms:]
    nodes = out.shape[0]
    total = refs[0][...].astype(F32)
    for ref in refs[1:terms]:
        total = total + ref[:nodes, :].astype(F32)
    out[...] = lax.dot_general(total.astype(BF16), weight[...], NT, preferred_element_type=F32).astype(BF16)


def feature_gradient(terms, weight):
    nodes, width = terms[0].shape
    depth = weight.shape[0]
    return pl.pallas_call(
        functools.partial(feature_kernel, len(terms)),
        out_shape=jax.ShapeDtypeStruct((nodes, depth), BF16),
        compiler_params=params(),
        cost_estimate=cost(2 * nodes * depth * width, 2 * nodes * width * (len(terms) + 2)),
        name="feature_gradient",
    )(*terms, weight)


def add(left, right):
    return (left.astype(F32) + right.astype(F32)).astype(BF16)


def shards(
    features,
    weight,
    bias_term,
    block_values,
    block_rows,
    block_cols,
    counts,
    cluster_order,
    cotangent,
):
    node_count, width = features.shape
    row_devices = lax.axis_size("row")
    col_devices = lax.axis_size("col")
    levels = col_devices // 2
    block = block_values.shape[3]
    row_blocks = node_count * col_devices // block

    row_masks = [1 << i for i in range((row_devices - 1).bit_length())]
    level_masks = [2 << i for i in reversed(range((levels - 1).bit_length()))]
    row_order, level_order = far_first(row_devices), far_first(levels)
    with jax.named_scope("gather_features"):
        pieces = exchange([features] * row_devices, "row", 1)
    tile, tile_turned, weight_near, bias_near, cotangent_near = prep(
        block_values[0, 0], block_rows, block_cols, counts, cluster_order, weight, bias_term, cotangent, row_blocks
    )

    with jax.named_scope("forward"):
        far, runs = ordered(pieces, row_order), runs_of(row_order, node_count)
        near = levels // 2
        (other_far,) = product(tile, far, runs, [node_count * (levels - near)], "forward_far", node_count * (levels + near))
        *kept, other_near = product(tile, far, runs, [node_count] * levels + [node_count * near], "forward_near")
        pairs = []
        for group, sent in ((kept[:near], other_near), (kept[near:], other_far)):
            arrived = swap(sent, "col", 1)
            pairs += [add(k, arrived[i * node_count : (i + 1) * node_count]) for i, k in enumerate(group)]
        terms = exchange(pairs, "col", 2)
        preact, slopes, weight_kept, weight_sent = slopes_of(
            ordered(terms, level_order), weight_near, bias_near, cotangent_near
        )
    activations = activation(preact)

    with jax.named_scope("gather_slopes"):
        slope_own = exchange([slopes] * levels, "col", 2)

    with jax.named_scope("weight_rows"):
        term = add(weight_kept, swap(weight_sent, "col", 1))
        for mask in row_masks:
            other = swap(term, "row", mask)
            if mask == row_masks[-1]:
                other, _ = lax.optimization_barrier((other, slope_own[1:]))
            term = add(term, other)

    with jax.named_scope("backward"):
        far = ordered(slope_own, level_order)
        slope_other = swap(jnp.concatenate(far), "col", 1)
        runs = runs_of(level_order, node_count)
        node_terms = product(
            tile_turned,
            far + [slope_other],
            runs + [(levels, part * node_count, node_count) for part, _, _ in runs],
            [node_count] * row_devices,
            "backward_tile",
        )
        node_sum = exchange(node_terms, "row", 1)
        grad_features = feature_gradient(ordered(node_sum, row_order), weight_near)

    with jax.named_scope("weight_levels"):
        for mask in level_masks[:-1]:
            term = add(term, swap(term, "col", mask))
        others = [swap(term, "col", mask) for mask in (level_masks[-1], level_masks[-1] | 1, 1)]
        others, _ = lax.optimization_barrier((others, grad_features))
        term, partner = add(term, others[0]), add(others[1], others[2])
        core = lax.axis_index("col") & 1
        scale = 1.0 / math.sqrt(node_count * row_devices * col_devices)
        both = jnp.where(
            core == 0, jnp.concatenate([term, partner]), jnp.concatenate([partner, term])
        )
        grad_weight = both.astype(F32) * scale
    return (activations, grad_features, grad_weight)


def solution(mesh):
    placed = (
        P(("col", "row"), None),
        P(),
        P(),
        P("row", "col", None, None, None),
        P("row", "col", None),
        P("row", "col", None),
        P("row", "col"),
        P("col"),
        P(("row", "col"), None),
    )
    return jax.shard_map(
        shards,
        mesh=mesh,
        in_specs=placed,
        out_specs=(P(("row", "col"), None), P(("col", "row"), None), P()),
        check_vma=False,
    )
```

```python
import functools
import math

import jax
import jax.numpy as jnp
from jax import lax
from jax.experimental import pallas as pl
from jax.experimental.pallas import tpu as pltpu
from jax.sharding import PartitionSpec as P

F32 = jnp.float32
BF16 = jnp.bfloat16
MIB = 1024 * 1024


def params(tile_bytes=0):
    return pltpu.CompilerParams(vmem_limit_bytes=(8 if tile_bytes <= MIB else 48) * MIB)


def cost(flops, nbytes, transcendentals=0):
    return pl.CostEstimate(flops=flops, bytes_accessed=nbytes, transcendentals=transcendentals)


def whole(shape):
    return pl.BlockSpec(shape, lambda *_: (0,) * len(shape))


def swap(value, axis, mask):
    size = lax.axis_size(axis)
    return lax.ppermute(value, axis, [(i, i ^ mask) for i in range(size)])


def swap_by_core(value, mask0, mask1):
    size = lax.axis_size("col")
    return lax.ppermute(value, "col", [(i, i ^ (mask1 if i & 1 else mask0)) for i in range(size)])


def exchange(values, axis, unit):
    out = list(values)
    for m in reversed(range(1, len(values))):
        out[m] = swap(values[m], axis, m * unit)
    return out


def far_first(count):
    return list(reversed(range(count)))


def ordered(values, order):
    return [values[i] for i in order]


def run(part, index, size, place0, place1=None):
    return (part, index * size, size, (place0 * size, (place0 if place1 is None else place1) * size))


def runs_of(order, size):
    return [run(i, 0, size, place) for i, place in enumerate(order)]


def tiled_dot(shape, store, lhs_rows, rhs_rows):
    rows, cols = shape
    row_step, col_step = min(rows, 512), min(cols, 512)

    def tile(i, j):
        left = lhs_rows(pl.multiple_of(i * row_step, row_step), row_step)
        right = rhs_rows(pl.multiple_of(j * col_step, col_step), col_step)
        return lax.dot_general(left, right, NT, preferred_element_type=F32)

    def step(t, carry):
        i, j = t // (cols // col_step), t % (cols // col_step)
        value = tile(i, j)
        rows_at = pl.ds(pl.multiple_of(i * row_step, row_step), row_step)
        store(rows_at, pl.ds(pl.multiple_of(j * col_step, col_step), col_step), value)
        return carry

    steps = (rows // row_step) * (cols // col_step)
    if steps <= 4:
        for t in range(steps):
            step(t, 0)
    else:
        lax.fori_loop(0, steps, step, 0)


NT = (((1,), (1,)), ((), ()))


def prep_kernel(
    per_step, count, rows_hbm, cols_hbm, order_hbm, values_hbm, weight_hbm, bias_hbm, cotangent_hbm,
    a_ref, at_ref, weight_ref, bias_ref, cotangent_ref,
    dense, select, values, order, rows, cols, sems,
):
    block = values.shape[1]
    nodes = select.shape[0]
    first = pl.program_id(0) * per_step
    row_blocks = pl.num_programs(0) * per_step
    row, col = lax.axis_index("row"), lax.axis_index("col")
    pairs = (
        (order_hbm, order), (rows_hbm, rows), (cols_hbm, cols), (values_hbm, values),
        (weight_hbm, weight_ref), (bias_hbm, bias_ref), (cotangent_hbm, cotangent_ref),
    )
    copies = [pltpu.make_async_copy(src, dst, sems.at[i]) for i, (src, dst) in enumerate(pairs)]
    once = pl.program_id(0) == 0

    @pl.when(once)
    def _():
        for copy in copies:
            copy.start()

    dense[...] = jnp.zeros_like(dense)

    @pl.when(once)
    def _():
        copies[0].wait()
        local = lax.broadcasted_iota(jnp.int32, (block, block), 0)
        for chunk in range(nodes // block):
            node = (row ^ chunk) * block + local
            for part in range(nodes // block):
                hit = order[part : part + 1, :] == node
                select[chunk * block : (chunk + 1) * block, part * block : (part + 1) * block] = jnp.where(
                    hit, 1.0, 0.0
                ).astype(BF16)
        for copy in copies[1:]:
            copy.wait()

    def slot(s, carry):
        turned = rows[0, 0, s] ^ col
        place = (turned & 1) * (row_blocks // 2) + (turned >> 1) - first

        @pl.when((place >= 0) & (place < per_step))
        def _():
            dense[
                pl.ds(pl.multiple_of(place * block, block), block),
                pl.ds(pl.multiple_of(cols[0, 0, s] * block, block), block),
            ] = values[s]

        return carry

    lax.fori_loop(0, count[0, 0], slot, 0)

    def store_a(i, j, value):
        a_ref[i, j] = value.astype(BF16)

    def store_at(i, j, value):
        at_ref[i, j] = value.astype(BF16)

    dense_rows = lambda i, n: dense[pl.ds(i, n), :]
    select_rows = lambda i, n: select[pl.ds(i, n), :]
    tiled_dot((per_step * block, nodes), store_a, dense_rows, select_rows)
    tiled_dot((nodes, per_step * block), store_at, select_rows, dense_rows)


def prep(values, rows, cols, count, order, weight, bias, cotangent, row_blocks):
    capacity, block, _ = values.shape
    nodes = order.shape[0]
    per_step = min(row_blocks, 8)
    order = order.reshape(nodes // block, block)
    bias = bias.reshape(1, bias.shape[0])
    passed = (weight, bias, cotangent)
    return pl.pallas_call(
        functools.partial(prep_kernel, per_step),
        grid=(row_blocks // per_step,),
        out_shape=(
            jax.ShapeDtypeStruct((row_blocks * block, nodes), BF16),
            jax.ShapeDtypeStruct((nodes, row_blocks * block), BF16),
        )
        + tuple(jax.ShapeDtypeStruct(p.shape, p.dtype) for p in passed),
        in_specs=[pl.BlockSpec(memory_space=pltpu.SMEM)] + [pl.BlockSpec(memory_space=pltpu.HBM)] * 7,
        out_specs=(
            pl.BlockSpec((per_step * block, nodes), lambda i: (i, 0)),
            pl.BlockSpec((nodes, per_step * block), lambda i: (0, i)),
        )
        + tuple(whole(p.shape) for p in passed),
        scratch_shapes=[
            pltpu.VMEM((per_step * block, nodes), BF16),
            pltpu.VMEM((nodes, nodes), BF16),
            pltpu.VMEM(values.shape, BF16),
            pltpu.VMEM(order.shape, jnp.int32),
            pltpu.SMEM(rows.shape, jnp.int32),
            pltpu.SMEM(cols.shape, jnp.int32),
            pltpu.SemaphoreType.DMA((7,)),
        ],
        compiler_params=params(2 * row_blocks * block * nodes),
        cost_estimate=cost(4 * row_blocks * block * nodes * nodes, 2 * values.size),
        name="prep",
    )(count, *(pltpu.with_memory_space_constraint(x, pltpu.HBM) for x in (rows, cols, order, values, *passed)))


def product_kernel(count, runs, top, *refs):
    matrix, parts, outs, joined = refs[0], refs[1 : 1 + count], refs[1 + count : -1], refs[-1]

    @pl.when(pl.program_id(0) == 0)
    def _():
        core = lax.axis_index("col") & 1
        for part, first, size, places in runs:
            start = jnp.where(core == 0, *places) if places[0] != places[1] else places[0]
            joined[pl.ds(pl.multiple_of(start, size), size), :] = parts[part][first : first + size, :]

    rows = sum(out.shape[0] for out in outs)
    total = lax.dot_general(
        matrix[top : top + rows, :], joined[...], (((1,), (0,)), ((), ())), preferred_element_type=F32
    )
    start = 0
    for out in outs:
        out[...] = total[start : start + out.shape[0]].astype(out.dtype)
        start += out.shape[0]


def product(matrix, parts, runs, sizes, name, top=0):
    rows, depth = sum(sizes), matrix.shape[1]
    width = parts[0].shape[1]
    small = matrix.size <= MIB
    if small:
        step = rows
        matrix_spec = whole(matrix.shape)
        out_shape = [jax.ShapeDtypeStruct((n, width), BF16) for n in sizes]
        out_specs = [whole((n, width)) for n in sizes]
    else:
        step = math.gcd(math.gcd(rows, top), 1024)
        matrix_spec = pl.BlockSpec((step, depth), lambda i: (top // step + i, 0))
        out_shape = [jax.ShapeDtypeStruct((rows, width), BF16)]
        out_specs = [pl.BlockSpec((step, width), lambda i: (i, 0))]
    outs = pl.pallas_call(
        functools.partial(product_kernel, len(parts), tuple(runs), top if small else 0),
        grid=(rows // step,),
        out_shape=out_shape,
        in_specs=[matrix_spec] + [whole(p.shape) for p in parts],
        out_specs=out_specs,
        scratch_shapes=[pltpu.VMEM((depth, width), BF16)],
        compiler_params=params(2 * matrix.size),
        cost_estimate=cost(2 * rows * depth * width, 2 * (rows * depth + depth * width + rows * width)),
        name=name,
    )(matrix, *parts)
    if small:
        return list(outs)
    cuts, start = [], 0
    for n in sizes:
        cuts.append(outs[0][start : start + n])
        start += n
    return cuts


def slopes_kernel(terms, *refs):
    weight, bias, cotangent = refs[terms : terms + 3]
    preact_ref, slopes, kept, sent, whole_term = refs[terms + 3 :]
    mixed = refs[0][...].astype(F32)
    for ref in refs[1:terms]:
        mixed = mixed + ref[...].astype(F32)
    high = mixed.astype(BF16)
    low = (mixed - high.astype(F32)).astype(BF16)
    preact = (
        jnp.dot(high, weight[...], preferred_element_type=F32)
        + jnp.dot(low, weight[...], preferred_element_type=F32)
        + bias[...]
    )
    preact_ref[...] = preact
    gate = 1.0 / (1.0 + jnp.exp(-preact))
    slope = (cotangent[...].astype(F32) * (gate * (1.0 + preact * (1.0 - gate)))).astype(BF16)
    slopes[...] = slope
    whole_term[...] = lax.dot_general(high, slope, (((0,), (0,)), ((), ())), preferred_element_type=F32)
    half = kept.shape[0]
    core = lax.axis_index("col") & 1
    kept[...] = whole_term[pl.ds(pl.multiple_of(core * half, half), half), :].astype(kept.dtype)
    sent[...] = whole_term[pl.ds(pl.multiple_of((1 - core) * half, half), half), :].astype(sent.dtype)


def slopes_of(terms, weight, bias, cotangent):
    nodes, width = cotangent.shape
    depth = weight.shape[0]
    half_out = jax.ShapeDtypeStruct((depth // 2, width), BF16)
    return pl.pallas_call(
        functools.partial(slopes_kernel, len(terms)),
        out_shape=(
            jax.ShapeDtypeStruct((nodes, width), F32),
            jax.ShapeDtypeStruct((nodes, width), BF16),
            half_out,
            half_out,
        ),
        scratch_shapes=[pltpu.VMEM((depth, width), F32)],
        compiler_params=params(),
        cost_estimate=cost(6 * nodes * depth * width, 2 * nodes * width * (len(terms) + 5), nodes * width),
        name="slopes",
    )(*terms, weight, bias, cotangent)


def activation_kernel(preact_ref, out):
    preact = preact_ref[...]
    out[...] = (preact / (1.0 + jnp.exp(-preact))).astype(BF16)


def activation(preact):
    return pl.pallas_call(
        activation_kernel,
        out_shape=jax.ShapeDtypeStruct(preact.shape, BF16),
        compiler_params=params(),
        cost_estimate=cost(4 * preact.size, 6 * preact.size, preact.size),
        name="activation",
    )(preact)


def feature_kernel(terms, *refs):
    weight, out = refs[terms:]
    nodes = out.shape[0]
    total = refs[0][...].astype(F32)
    for ref in refs[1:terms]:
        total = total + ref[:nodes, :].astype(F32)
    out[...] = lax.dot_general(total.astype(BF16), weight[...], NT, preferred_element_type=F32).astype(BF16)


def feature_gradient(terms, weight):
    nodes, width = terms[0].shape
    depth = weight.shape[0]
    return pl.pallas_call(
        functools.partial(feature_kernel, len(terms)),
        out_shape=jax.ShapeDtypeStruct((nodes, depth), BF16),
        compiler_params=params(),
        cost_estimate=cost(2 * nodes * depth * width, 2 * nodes * width * (len(terms) + 2)),
        name="feature_gradient",
    )(*terms, weight)


def add(left, right):
    return (left.astype(F32) + right.astype(F32)).astype(BF16)


def add_all(values):
    return sum(value.astype(F32) for value in values).astype(BF16)


def shards(
    features,
    weight,
    bias_term,
    block_values,
    block_rows,
    block_cols,
    counts,
    cluster_order,
    cotangent,
):
    node_count, width = features.shape
    row_devices = lax.axis_size("row")
    col_devices = lax.axis_size("col")
    levels = col_devices // 2
    block = block_values.shape[3]
    row_blocks = node_count * col_devices // block

    level_masks = [2 << i for i in reversed(range((levels - 1).bit_length()))]
    row_order, level_order = far_first(row_devices), far_first(levels)
    with jax.named_scope("gather_features"):
        pieces = exchange([features] * row_devices, "row", 1)
    tile, tile_turned, weight_near, bias_near, cotangent_near = prep(
        block_values[0, 0], block_rows, block_cols, counts, cluster_order, weight, bias_term, cotangent, row_blocks
    )

    with jax.named_scope("forward"):
        far, runs = ordered(pieces, row_order), runs_of(row_order, node_count)
        near = levels // 2
        (other_far,) = product(tile, far, runs, [node_count * (levels - near)], "forward_far", node_count * (levels + near))
        *kept, other_near = product(tile, far, runs, [node_count] * levels + [node_count * near], "forward_near")
        pairs = []
        for group, sent in ((kept[:near], other_near), (kept[near:], other_far)):
            arrived = swap(sent, "col", 1)
            pairs += [add(k, arrived[i * node_count : (i + 1) * node_count]) for i, k in enumerate(group)]
        terms = exchange(pairs, "col", 2)
        preact, slopes, weight_kept, weight_sent = slopes_of(
            ordered(terms, level_order), weight_near, bias_near, cotangent_near
        )
    activations = activation(preact)

    with jax.named_scope("gather_slopes"):
        arrived = swap(jnp.concatenate([slopes, weight_sent]), "col", 1)
        both = jnp.concatenate([slopes, arrived[:node_count]])
        far_pairs = [(m, m - 1) for m in range(levels - 1, 1, -2)]
        far = [swap_by_core(both, 2 * m0, 2 * m1) for m0, m1 in far_pairs]
        near = swap(slopes, "col", 2)

    with jax.named_scope("weight_rows"):
        term = add(weight_kept, arrived[node_count:])
        step = 1
        while step < row_devices:
            wide = min(4, row_devices // step)
            others = [swap(term, "row", m * step) for m in reversed(range(1, wide))]
            step *= wide
            if step == row_devices:
                others, _ = lax.optimization_barrier((others, (far, near)))
            term = add_all([term] + others)

    with jax.named_scope("backward"):
        handed = swap(jnp.concatenate(far + [near]), "col", 1)
        runs = [run(0, 0, node_count, 0), run(1, 0, node_count, levels), run(2 + len(far), 0, node_count, 1)]
        for i, (m0, m1) in enumerate(far_pairs):
            runs += [run(2 + i, 0, node_count, m0, m1), run(2 + i, 1, node_count, levels + m0, levels + m1)]
            runs += [run(3 + len(far), 2 * i, node_count, levels + m1, levels + m0), run(3 + len(far), 2 * i + 1, node_count, m1, m0)]
        runs.append(run(3 + len(far), 2 * len(far), node_count, levels + 1))
        node_terms = product(
            tile_turned,
            [slopes, arrived] + far + [near, handed],
            runs,
            [node_count] * row_devices,
            "backward_tile",
        )
        node_sum = exchange(node_terms, "row", 1)
        grad_features = feature_gradient(ordered(node_sum, row_order), weight_near)

    with jax.named_scope("weight_levels"):
        for mask in level_masks[:-1]:
            term = add(term, swap(term, "col", mask))
        others = [swap(term, "col", mask) for mask in (level_masks[-1], level_masks[-1] | 1, 1)]
        others, _ = lax.optimization_barrier((others, grad_features))
        term, partner = add(term, others[0]), add(others[1], others[2])
        core = lax.axis_index("col") & 1
        scale = 1.0 / math.sqrt(node_count * row_devices * col_devices)
        both = jnp.where(
            core == 0, jnp.concatenate([term, partner]), jnp.concatenate([partner, term])
        )
        grad_weight = both.astype(F32) * scale
    return (activations, grad_features, grad_weight)


def solution(mesh):
    placed = (
        P(("col", "row"), None),
        P(),
        P(),
        P("row", "col", None, None, None),
        P("row", "col", None),
        P("row", "col", None),
        P("row", "col"),
        P("col"),
        P(("row", "col"), None),
    )
    return jax.shard_map(
        shards,
        mesh=mesh,
        in_specs=placed,
        out_specs=(P(("row", "col"), None), P(("col", "row"), None), P()),
        check_vma=False,
    )
```

```python
import functools
import math

import jax
import jax.numpy as jnp
from jax import lax
from jax.experimental import pallas as pl
from jax.experimental.pallas import tpu as pltpu
from jax.sharding import PartitionSpec as P

F32 = jnp.float32
BF16 = jnp.bfloat16
MIB = 1024 * 1024


def params(tile_bytes=0):
    return pltpu.CompilerParams(vmem_limit_bytes=(8 if tile_bytes <= MIB else 48) * MIB)


def cost(flops, nbytes, transcendentals=0):
    return pl.CostEstimate(flops=flops, bytes_accessed=nbytes, transcendentals=transcendentals)


def whole(shape):
    return pl.BlockSpec(shape, lambda *_: (0,) * len(shape))


def swap(value, axis, mask):
    size = lax.axis_size(axis)
    return lax.ppermute(value, axis, [(i, i ^ mask) for i in range(size)])


def swap_by_core(value, mask0, mask1):
    size = lax.axis_size("col")
    return lax.ppermute(value, "col", [(i, i ^ (mask1 if i & 1 else mask0)) for i in range(size)])


def exchange(values, axis, unit):
    out = list(values)
    for m in reversed(range(1, len(values))):
        out[m] = swap(values[m], axis, m * unit)
    return out


def far_first(count):
    return list(reversed(range(count)))


def ordered(values, order):
    return [values[i] for i in order]


def run(part, index, size, place0, place1=None):
    return (part, index * size, size, (place0 * size, (place0 if place1 is None else place1) * size))


def runs_of(order, size):
    return [run(i, 0, size, place) for i, place in enumerate(order)]


def tiled_dot(shape, store, lhs_rows, rhs_rows):
    rows, cols = shape
    row_step, col_step = min(rows, 512), min(cols, 512)

    def tile(i, j):
        left = lhs_rows(pl.multiple_of(i * row_step, row_step), row_step)
        right = rhs_rows(pl.multiple_of(j * col_step, col_step), col_step)
        return lax.dot_general(left, right, NT, preferred_element_type=F32)

    def step(t, carry):
        i, j = t // (cols // col_step), t % (cols // col_step)
        value = tile(i, j)
        rows_at = pl.ds(pl.multiple_of(i * row_step, row_step), row_step)
        store(rows_at, pl.ds(pl.multiple_of(j * col_step, col_step), col_step), value)
        return carry

    steps = (rows // row_step) * (cols // col_step)
    if steps <= 4:
        for t in range(steps):
            step(t, 0)
    else:
        lax.fori_loop(0, steps, step, 0)


NT = (((1,), (1,)), ((), ()))


def prep_kernel(
    per_step, count, rows_hbm, cols_hbm, order_hbm, values_hbm, weight_hbm, bias_hbm, cotangent_hbm,
    a_ref, at_ref, weight_ref, bias_ref, cotangent_ref,
    dense, select, values, order, rows, cols, sems,
):
    block = values.shape[1]
    nodes = select.shape[0]
    first = pl.program_id(0) * per_step
    row_blocks = pl.num_programs(0) * per_step
    row, col = lax.axis_index("row"), lax.axis_index("col")
    pairs = (
        (order_hbm, order), (rows_hbm, rows), (cols_hbm, cols), (values_hbm, values),
        (weight_hbm, weight_ref), (bias_hbm, bias_ref), (cotangent_hbm, cotangent_ref),
    )
    copies = [pltpu.make_async_copy(src, dst, sems.at[i]) for i, (src, dst) in enumerate(pairs)]
    once = pl.program_id(0) == 0

    @pl.when(once)
    def _():
        for copy in copies:
            copy.start()

    dense[...] = jnp.zeros_like(dense)

    @pl.when(once)
    def _():
        copies[0].wait()
        local = lax.broadcasted_iota(jnp.int32, (block, block), 0)
        for chunk in range(nodes // block):
            node = (row ^ chunk) * block + local
            for part in range(nodes // block):
                hit = order[part : part + 1, :] == node
                select[chunk * block : (chunk + 1) * block, part * block : (part + 1) * block] = jnp.where(
                    hit, 1.0, 0.0
                ).astype(BF16)
        for copy in copies[1:]:
            copy.wait()

    def slot(s, carry):
        turned = rows[0, 0, s] ^ col
        place = (turned & 1) * (row_blocks // 2) + (turned >> 1) - first

        @pl.when((place >= 0) & (place < per_step))
        def _():
            dense[
                pl.ds(pl.multiple_of(place * block, block), block),
                pl.ds(pl.multiple_of(cols[0, 0, s] * block, block), block),
            ] = values[s]

        return carry

    lax.fori_loop(0, count[0, 0], slot, 0)

    def store_a(i, j, value):
        a_ref[i, j] = value.astype(BF16)

    def store_at(i, j, value):
        at_ref[i, j] = value.astype(BF16)

    dense_rows = lambda i, n: dense[pl.ds(i, n), :]
    select_rows = lambda i, n: select[pl.ds(i, n), :]
    tiled_dot((per_step * block, nodes), store_a, dense_rows, select_rows)
    tiled_dot((nodes, per_step * block), store_at, select_rows, dense_rows)


def prep(values, rows, cols, count, order, weight, bias, cotangent, row_blocks):
    capacity, block, _ = values.shape
    nodes = order.shape[0]
    per_step = min(row_blocks, 8)
    order = order.reshape(nodes // block, block)
    bias = bias.reshape(1, bias.shape[0])
    passed = (weight, bias, cotangent)
    return pl.pallas_call(
        functools.partial(prep_kernel, per_step),
        grid=(row_blocks // per_step,),
        out_shape=(
            jax.ShapeDtypeStruct((row_blocks * block, nodes), BF16),
            jax.ShapeDtypeStruct((nodes, row_blocks * block), BF16),
        )
        + tuple(jax.ShapeDtypeStruct(p.shape, p.dtype) for p in passed),
        in_specs=[pl.BlockSpec(memory_space=pltpu.SMEM)] + [pl.BlockSpec(memory_space=pltpu.HBM)] * 7,
        out_specs=(
            pl.BlockSpec((per_step * block, nodes), lambda i: (i, 0)),
            pl.BlockSpec((nodes, per_step * block), lambda i: (0, i)),
        )
        + tuple(whole(p.shape) for p in passed),
        scratch_shapes=[
            pltpu.VMEM((per_step * block, nodes), BF16),
            pltpu.VMEM((nodes, nodes), BF16),
            pltpu.VMEM(values.shape, BF16),
            pltpu.VMEM(order.shape, jnp.int32),
            pltpu.SMEM(rows.shape, jnp.int32),
            pltpu.SMEM(cols.shape, jnp.int32),
            pltpu.SemaphoreType.DMA((7,)),
        ],
        compiler_params=params(2 * row_blocks * block * nodes),
        cost_estimate=cost(4 * row_blocks * block * nodes * nodes, 2 * values.size),
        name="prep",
    )(count, *(pltpu.with_memory_space_constraint(x, pltpu.HBM) for x in (rows, cols, order, values, *passed)))


def product_kernel(count, runs, top, *refs):
    matrix, parts, outs, joined = refs[0], refs[1 : 1 + count], refs[1 + count : -1], refs[-1]

    @pl.when(pl.program_id(0) == 0)
    def _():
        core = lax.axis_index("col") & 1
        for part, first, size, places in runs:
            start = jnp.where(core == 0, *places) if places[0] != places[1] else places[0]
            joined[pl.ds(pl.multiple_of(start, size), size), :] = parts[part][first : first + size, :]

    rows = sum(out.shape[0] for out in outs)
    total = lax.dot_general(
        matrix[top : top + rows, :], joined[...], (((1,), (0,)), ((), ())), preferred_element_type=F32
    )
    start = 0
    for out in outs:
        out[...] = total[start : start + out.shape[0]].astype(out.dtype)
        start += out.shape[0]


def product(matrix, parts, runs, sizes, name, top=0):
    rows, depth = sum(sizes), matrix.shape[1]
    width = parts[0].shape[1]
    small = matrix.size <= MIB
    if small:
        step = rows
        matrix_spec = whole(matrix.shape)
        out_shape = [jax.ShapeDtypeStruct((n, width), BF16) for n in sizes]
        out_specs = [whole((n, width)) for n in sizes]
    else:
        step = math.gcd(math.gcd(rows, top), 1024)
        matrix_spec = pl.BlockSpec((step, depth), lambda i: (top // step + i, 0))
        out_shape = [jax.ShapeDtypeStruct((rows, width), BF16)]
        out_specs = [pl.BlockSpec((step, width), lambda i: (i, 0))]
    outs = pl.pallas_call(
        functools.partial(product_kernel, len(parts), tuple(runs), top if small else 0),
        grid=(rows // step,),
        out_shape=out_shape,
        in_specs=[matrix_spec] + [whole(p.shape) for p in parts],
        out_specs=out_specs,
        scratch_shapes=[pltpu.VMEM((depth, width), BF16)],
        compiler_params=params(2 * matrix.size),
        cost_estimate=cost(2 * rows * depth * width, 2 * (rows * depth + depth * width + rows * width)),
        name=name,
    )(matrix, *parts)
    if small:
        return list(outs)
    cuts, start = [], 0
    for n in sizes:
        cuts.append(outs[0][start : start + n])
        start += n
    return cuts


def slopes_kernel(terms, *refs):
    weight, bias, cotangent = refs[terms : terms + 3]
    preact_ref, slopes, kept, sent, whole_term = refs[terms + 3 :]
    mixed = refs[0][...].astype(F32)
    for ref in refs[1:terms]:
        mixed = mixed + ref[...].astype(F32)
    high = mixed.astype(BF16)
    low = (mixed - high.astype(F32)).astype(BF16)
    preact = (
        jnp.dot(high, weight[...], preferred_element_type=F32)
        + jnp.dot(low, weight[...], preferred_element_type=F32)
        + bias[...]
    )
    preact_ref[...] = preact
    gate = 1.0 / (1.0 + jnp.exp(-preact))
    slope = (cotangent[...].astype(F32) * (gate * (1.0 + preact * (1.0 - gate)))).astype(BF16)
    slopes[...] = slope
    whole_term[...] = lax.dot_general(high, slope, (((0,), (0,)), ((), ())), preferred_element_type=F32)
    half = kept.shape[0]
    core = lax.axis_index("col") & 1
    kept[...] = whole_term[pl.ds(pl.multiple_of(core * half, half), half), :].astype(kept.dtype)
    sent[...] = whole_term[pl.ds(pl.multiple_of((1 - core) * half, half), half), :].astype(sent.dtype)


def slopes_of(terms, weight, bias, cotangent):
    nodes, width = cotangent.shape
    depth = weight.shape[0]
    half_out = jax.ShapeDtypeStruct((depth // 2, width), BF16)
    return pl.pallas_call(
        functools.partial(slopes_kernel, len(terms)),
        out_shape=(
            jax.ShapeDtypeStruct((nodes, width), F32),
            jax.ShapeDtypeStruct((nodes, width), BF16),
            half_out,
            half_out,
        ),
        scratch_shapes=[pltpu.VMEM((depth, width), F32)],
        compiler_params=params(),
        cost_estimate=cost(6 * nodes * depth * width, 2 * nodes * width * (len(terms) + 5), nodes * width),
        name="slopes",
    )(*terms, weight, bias, cotangent)


def activation_kernel(preact_ref, out):
    preact = preact_ref[...]
    out[...] = (preact / (1.0 + jnp.exp(-preact))).astype(BF16)


def activation(preact):
    return pl.pallas_call(
        activation_kernel,
        out_shape=jax.ShapeDtypeStruct(preact.shape, BF16),
        compiler_params=params(),
        cost_estimate=cost(4 * preact.size, 6 * preact.size, preact.size),
        name="activation",
    )(preact)


def feature_kernel(terms, *refs):
    weight, out = refs[terms:]
    nodes = out.shape[0]
    total = refs[0][...].astype(F32)
    for ref in refs[1:terms]:
        total = total + ref[:nodes, :].astype(F32)
    out[...] = lax.dot_general(total.astype(BF16), weight[...], NT, preferred_element_type=F32).astype(BF16)


def feature_gradient(terms, weight):
    nodes, width = terms[0].shape
    depth = weight.shape[0]
    return pl.pallas_call(
        functools.partial(feature_kernel, len(terms)),
        out_shape=jax.ShapeDtypeStruct((nodes, depth), BF16),
        compiler_params=params(),
        cost_estimate=cost(2 * nodes * depth * width, 2 * nodes * width * (len(terms) + 2)),
        name="feature_gradient",
    )(*terms, weight)


def add(left, right):
    return (left.astype(F32) + right.astype(F32)).astype(BF16)


def add_all(values):
    return sum(value.astype(F32) for value in values).astype(BF16)


def shards(
    features,
    weight,
    bias_term,
    block_values,
    block_rows,
    block_cols,
    counts,
    cluster_order,
    cotangent,
):
    node_count, width = features.shape
    row_devices = lax.axis_size("row")
    col_devices = lax.axis_size("col")
    levels = col_devices // 2
    block = block_values.shape[3]
    row_blocks = node_count * col_devices // block

    level_masks = [(4 << i) - 2 for i in reversed(range((levels - 1).bit_length()))]
    row_order, level_order = far_first(row_devices), far_first(levels)
    with jax.named_scope("gather_features"):
        pieces = exchange([features] * row_devices, "row", 1)
    tile, tile_turned, weight_near, bias_near, cotangent_near = prep(
        block_values[0, 0], block_rows, block_cols, counts, cluster_order, weight, bias_term, cotangent, row_blocks
    )

    with jax.named_scope("forward"):
        far, runs = ordered(pieces, row_order), runs_of(row_order, node_count)
        near = levels // 2
        (other_far,) = product(tile, far, runs, [node_count * (levels - near)], "forward_far", node_count * (levels + near))
        *kept, other_near = product(tile, far, runs, [node_count] * levels + [node_count * near], "forward_near")
        pairs = []
        for group, sent in ((kept[:near], other_near), (kept[near:], other_far)):
            arrived = swap(sent, "col", 1)
            pairs += [add(k, arrived[i * node_count : (i + 1) * node_count]) for i, k in enumerate(group)]
        terms = exchange(pairs, "col", 2)
        preact, slopes, weight_kept, weight_sent = slopes_of(
            ordered(terms, level_order), weight_near, bias_near, cotangent_near
        )
    activations = activation(preact)

    with jax.named_scope("gather_slopes"):
        arrived = swap(jnp.concatenate([slopes, weight_sent]), "col", 1)
        both = jnp.concatenate([slopes, arrived[:node_count]])
        far_pairs = [(m - 1, m) for m in range(levels - 1, 1, -2)]
        far = [swap_by_core(both, 2 * m0, 2 * m1) for m0, m1 in far_pairs]
        near = swap(slopes, "col", 2)

    with jax.named_scope("weight_rows"):
        term = add(weight_kept, arrived[node_count:])
        step = 1
        while step < row_devices:
            wide = min(4, row_devices // step)
            others = [swap(term, "row", m * step) for m in reversed(range(1, wide))]
            step *= wide
            if step == row_devices:
                others, _ = lax.optimization_barrier((others, (far, near)))
            term = add_all([term] + others)

    with jax.named_scope("backward"):
        handed = swap(jnp.concatenate(far + [near]), "col", 1)
        runs = [run(0, 0, node_count, 0), run(1, 0, node_count, levels), run(2 + len(far), 0, node_count, 1)]
        for i, (m0, m1) in enumerate(far_pairs):
            runs += [run(2 + i, 0, node_count, m0, m1), run(2 + i, 1, node_count, levels + m0, levels + m1)]
            runs += [run(3 + len(far), 2 * i, node_count, levels + m1, levels + m0), run(3 + len(far), 2 * i + 1, node_count, m1, m0)]
        runs.append(run(3 + len(far), 2 * len(far), node_count, levels + 1))
        node_terms = product(
            tile_turned,
            [slopes, arrived] + far + [near, handed],
            runs,
            [node_count] * row_devices,
            "backward_tile",
        )
        node_sum = exchange(node_terms, "row", 1)
        grad_features = feature_gradient(ordered(node_sum, row_order), weight_near)

    with jax.named_scope("weight_levels"):
        for mask in level_masks[:-1]:
            term = add(term, swap(term, "col", mask))
        others = [swap(term, "col", mask) for mask in (level_masks[-1], level_masks[-1] | 1, 1)]
        others, _ = lax.optimization_barrier((others, grad_features))
        term, partner = add(term, others[0]), add(others[1], others[2])
        core = lax.axis_index("col") & 1
        scale = 1.0 / math.sqrt(node_count * row_devices * col_devices)
        both = jnp.where(
            core == 0, jnp.concatenate([term, partner]), jnp.concatenate([partner, term])
        )
        grad_weight = both.astype(F32) * scale
    return (activations, grad_features, grad_weight)


def solution(mesh):
    placed = (
        P(("col", "row"), None),
        P(),
        P(),
        P("row", "col", None, None, None),
        P("row", "col", None),
        P("row", "col", None),
        P("row", "col"),
        P("col"),
        P(("row", "col"), None),
    )
    return jax.shard_map(
        shards,
        mesh=mesh,
        in_specs=placed,
        out_specs=(P(("row", "col"), None), P(("col", "row"), None), P()),
        check_vma=False,
    )
```
